256 devices in a mesh: row: 32 (over x, y, core), col: 8 (over z).
Axes of the slice: x: 4, y: 4, z: 8, core: 2. Of those that a mesh axis runs over, the one named last changes fastest.
Arguments:
- tokens: bfloat16 [512, 8192], P('row', 'col'), may hold values from -6 to 6
- gate_up: bfloat16 [8192, 2, 28672], P('col', None, 'row'), may hold values from -0.0625 to 0.0625
- down: bfloat16 [28672, 8192], P('row', 'col'), may hold values from -0.03125 to 0.03125
- target: bfloat16 [512, 8192], P('row', 'col'), may hold values from -6 to 6
Outputs:
- output: bfloat16 [512, 8192], P('row', 'col')
- grad_tokens: bfloat16 [512, 8192], P('row', 'col')
- grad_gate_up: bfloat16 [8192, 2, 28672], P('col', None, 'row')
- grad_down: bfloat16 [28672, 8192], P('row', 'col')
The draws below stay inside these ranges and needn't reach their ends.
All inputs are finite; a program needn't handle non-finite values.
Results may differ from the reference program's by a relative error of at most 0.04.
Values may be sent and summed in bfloat16 or wider, within the bound.
No kernel may reach another device: no remote copies, remote signals or barrier semaphores. Data moves between devices by JAX's collectives and lax.ppermute only.
A program may use at most 64 MiB of HBM per device.

```python
import jax
import jax.numpy as jnp
from jax import lax

D = 8192
FF = 28672
TOKENS = 512
N_COL = 8


def block_scale(rng, extent, split, least, high):
    factor_of = 1.0
    for axis_at, parts in split:
        draws = jax.random.uniform(jax.random.fold_in(jax.random.fold_in(rng, 6), axis_at), (parts,), jnp.float32, least / len(split), high / len(split))
        factor_of = factor_of * jnp.repeat(jnp.exp(draws), extent[axis_at] // parts).reshape((-1,) + (1,) * (len(extent) - 1 - axis_at))
    return factor_of


def centred(stream_key, extent, scale, bound, pieces=(), kind=jnp.bfloat16):
    factor_of = block_scale(stream_key, extent, pieces, -0.22, 0.18) if pieces else 1.0
    values = jax.random.normal(stream_key, extent, jnp.float32) * scale * factor_of
    return jnp.minimum(jnp.maximum(values, -bound), bound).astype(kind)


def setup_inputs(seed: int = 0) -> dict:
    key_of = jax.random.split(jax.random.key(seed), 5)
    return {
        "tokens": centred(key_of[0], (TOKENS, D), 1.0, 6.0, ((0, 32), (1, 8))),
        "gate_up": centred(key_of[1], (D, 2, FF), D ** -0.5, 0.0625, ((0, 8), (2, 32))),
        "down": centred(key_of[2], (FF, D), FF ** -0.5, 0.03125, ((0, 32), (1, 8))),
        "target": centred(key_of[3], (TOKENS, D), 1.0, 6.0, ((0, 32), (1, 8))),
    }


def blocked_sum(left, right, col_width):
    total = None
    for block in range(N_COL):
        start = block * col_width
        term = jnp.dot(left[:, start:start + col_width], right[start:start + col_width], preferred_element_type=jnp.float32)
        term = lax.optimization_barrier(term.astype(jnp.bfloat16)).astype(jnp.float32)
        total = term if total is None else total + term
    return total

def swiglu_grad(grad_hidden, gate, up):
    sigma = jax.nn.sigmoid(gate)
    grad_gate = grad_hidden * up * sigma * (1.0 + gate * (1.0 - sigma))
    grad_up = grad_hidden * gate * sigma
    return jnp.stack([grad_gate, grad_up], axis=1).astype(jnp.bfloat16)

def reference(tokens, gate_up, down, target):
    col_width = D // N_COL
    flat_weight = gate_up.reshape(D, 2 * FF)
    projected = blocked_sum(tokens, flat_weight, col_width).reshape(TOKENS, 2, FF)
    gate = projected[:, 0]
    up = projected[:, 1]
    hidden = (jax.nn.silu(gate) * up).astype(jnp.bfloat16)
    mixed = jnp.dot(hidden, down, preferred_element_type=jnp.float32)
    output = (tokens.astype(jnp.float32) + mixed).astype(jnp.bfloat16)
    delta = (output.astype(jnp.float32) - target.astype(jnp.float32)).astype(jnp.bfloat16)
    grad_hidden = blocked_sum(delta, down.T, col_width)
    grad_projected = swiglu_grad(grad_hidden, gate, up)
    grad_down = jnp.dot(hidden.T, delta, preferred_element_type=jnp.float32).astype(jnp.bfloat16)
    flat_grad = grad_projected.reshape(TOKENS, 2 * FF)
    grad_gate_up = jnp.dot(tokens.T, flat_grad, preferred_element_type=jnp.float32).astype(jnp.bfloat16).reshape(D, 2, FF)
    grad_inner = jnp.dot(flat_grad, flat_weight.T, preferred_element_type=jnp.float32)
    grad_tokens = (delta.astype(jnp.float32) + grad_inner).astype(jnp.bfloat16)
    return (output, grad_tokens, grad_gate_up, grad_down)
```

```python
import jax
import jax.numpy as jnp
from jax import lax
from jax.sharding import Mesh
from jax.sharding import PartitionSpec as P

BF16 = jnp.bfloat16
F32 = jnp.float32
ROW = ("x", "y", "core")
SIDE = 4
RING = 8


def fetch(value, axis, size, offset):
    return lax.ppermute(value, axis, [((i + offset) % size, i) for i in range(size)])


def swap_core(value):
    return lax.ppermute(value, "core", [(0, 1), (1, 0)])


def gather_rows(value):
    line = jnp.concatenate([value] + [fetch(value, "x", SIDE, k) for k in (1, 2, 3)], 0)
    own = jnp.concatenate([line] + [fetch(line, "y", SIDE, k) for k in (1, 2, 3)], 0)
    return own, swap_core(own)


def scatter_rows(own, other):
    got = swap_core(jnp.concatenate([b.astype(BF16) for b in other], 0))
    rows = own[0].shape[0]
    total = [b.astype(F32) + got[k * rows:(k + 1) * rows].astype(F32) for k, b in enumerate(own)]
    got = [fetch(total[k].astype(BF16), "y", SIDE, -k) for k in (1, 2, 3)]
    mine = total[0] + sum(g.astype(F32) for g in got)
    rows = rows // SIDE
    got = [fetch(mine[k * rows:(k + 1) * rows].astype(BF16), "x", SIDE, -k) for k in (1, 2, 3)]
    return mine[:rows] + sum(g.astype(F32) for g in got)


def add(a, b):
    return (a.astype(F32) + b.astype(F32)).astype(BF16)


def scatter_cols(parts):
    me = lax.axis_index("col")
    rows = parts[0].shape[0] // RING
    half = rows // 2

    def block(part, offset, start=0, count=rows):
        return lax.dynamic_slice_in_dim(part, lax.rem(me + offset + RING, RING) * rows + start, count, 0)

    up = [fetch(block(p, 4, 0, half), "col", RING, -1) for p in parts]
    down = [fetch(block(p, 4, half, half), "col", RING, 1) for p in parts]
    next_up, next_down = [], []
    for p, u, d in zip(parts, up, down):
        a, b = block(p, 3), block(p, -3)
        next_up.append(fetch(jnp.concatenate([add(a[:half], u), a[half:]], 0), "col", RING, -1))
        next_down.append(fetch(jnp.concatenate([b[:half], add(b[half:], d)], 0), "col", RING, 1))
    up, down = next_up, next_down
    for k in (2, 1):
        up = [fetch(add(block(p, k), u), "col", RING, -1) for p, u in zip(parts, up)]
        down = [fetch(add(block(p, -k), d), "col", RING, 1) for p, d in zip(parts, down)]
    return [
        block(p, 0).astype(F32) + u.astype(F32) + d.astype(F32) for p, u, d in zip(parts, up, down)
    ]


def gather_cols(values):
    half = values[0].shape[0] // 2
    ups, downs = [[v] for v in values], [[v] for v in values]
    for _ in range(3):
        for u, d in zip(ups, downs):
            u.append(fetch(u[-1], "col", RING, 1))
            d.append(fetch(d[-1], "col", RING, -1))
    out = []
    for u, d in zip(ups, downs):
        far = [fetch(u[3][:half], "col", RING, 1), fetch(d[3][half:], "col", RING, -1)]
        out.append(jnp.concatenate(u + far + [d[3], d[2], d[1]], 0))
    return out


def turn(value, rows):
    me = lax.axis_index("col")
    return lax.dynamic_slice_in_dim(jnp.concatenate([value, value], 0), me * rows, value.shape[0], 0)


def dy_blocks(value, rows):
    me = lax.axis_index("col")
    out = [
        lax.dynamic_slice_in_dim(value, lax.rem(j - me + RING, RING) * rows, rows, 0) for j in range(RING)
    ]
    return out[:SIDE], out[SIDE:]


def per_device(tokens, gate_up, down, target):
    all_tokens = jnp.concatenate(gather_rows(tokens), 0)
    rows = all_tokens.shape[0] // RING
    partial_value = jnp.einsum("td,dgf->gtf", all_tokens, gate_up, preferred_element_type=F32).astype(BF16)
    gate, up = scatter_cols([partial_value[0], partial_value[1]])
    sigma = jax.nn.sigmoid(gate)
    hidden = (gate * sigma * up).astype(BF16)
    (all_hidden,) = gather_cols([hidden])
    mixed = jnp.dot(all_hidden, down, preferred_element_type=F32).astype(BF16)
    mixed = scatter_rows(*dy_blocks(mixed, rows))
    output = (tokens.astype(F32) + mixed).astype(BF16)
    delta = (output.astype(F32) - target.astype(F32)).astype(BF16)
    all_delta = jnp.concatenate(gather_rows(delta), 0)
    hidden_part = jnp.einsum("td,fd->tf", all_delta, down, preferred_element_type=F32).astype(BF16)
    (grad_hidden,) = scatter_cols([hidden_part])
    grad_down = jnp.einsum(
        "tf,td->fd", all_hidden, turn(all_delta, rows), preferred_element_type=F32
    ).astype(BF16)
    grad_gate = (grad_hidden * up * sigma * (1.0 + gate * (1.0 - sigma))).astype(BF16)
    grad_up = (grad_hidden * gate * sigma).astype(BF16)
    all_grad = jnp.stack(gather_cols([grad_gate, grad_up]), 0)
    inner = jnp.einsum("gtf,dgf->td", all_grad, gate_up, preferred_element_type=F32).astype(BF16)
    grad_inner = scatter_rows(*dy_blocks(inner, rows))
    grad_gate_up = jnp.einsum(
        "td,gtf->dgf", turn(all_tokens, rows), all_grad, preferred_element_type=F32
    ).astype(BF16)
    grad_tokens = (delta.astype(F32) + grad_inner).astype(BF16)
    return (output, grad_tokens, grad_gate_up, grad_down)


def solution(mesh):
    chips = Mesh(mesh.devices.reshape(SIDE, SIDE, 2, RING), ROW + ("col",))
    in_specs = (P(ROW, "col"), P("col", None, ROW), P(ROW, "col"), P(ROW, "col"))
    out_specs = (P(ROW, "col"), P(ROW, "col"), P("col", None, ROW), P(ROW, "col"))
    return jax.shard_map(
        per_device, mesh=chips, in_specs=in_specs, out_specs=out_specs, check_vma=False
    )
```

```python
import jax
import jax.numpy as jnp
from jax import lax
from jax.sharding import Mesh
from jax.sharding import PartitionSpec as P

BF16 = jnp.bfloat16
F32 = jnp.float32
ROW = ("x", "y", "core")
PLANE = ("x", "y")
SIDE = 4
RING = 8


def fetch(value, axis, size, offset):
    return lax.ppermute(value, axis, [((i + offset) % size, i) for i in range(size)])


def swap_core(value):
    return lax.ppermute(value, "core", [(0, 1), (1, 0)])


def gather(value, axes, size):
    copies = jnp.broadcast_to(value[None], (size,) + value.shape).reshape((-1,) + value.shape[1:])
    return lax.all_to_all(copies, axes, 0, 0, tiled=True)


def gather_rows(value):
    own = gather(value, PLANE, SIDE * SIDE)
    return jnp.concatenate([own, swap_core(own)], 0)


def scatter_rows(own, other):
    total = (own + swap_core(other.astype(BF16)).astype(F32)).astype(BF16)
    got = lax.all_to_all(total, PLANE, 0, 0, tiled=True)
    return jnp.sum(got.reshape((SIDE * SIDE, -1) + got.shape[1:]).astype(F32), 0)


def scatter_rows_in_steps(own, other):
    total = own + swap_core(other.astype(BF16)).astype(F32)
    total = total.astype(BF16).reshape((SIDE, SIDE, -1) + total.shape[1:])
    x, y = lax.axis_index("x"), lax.axis_index("y")

    def pick(value, axis, at, offset):
        return lax.dynamic_index_in_dim(value, lax.rem(at + offset, SIDE), axis, False)

    got = [fetch(pick(total, 1, y, k), "y", SIDE, -k) for k in (1, 2, 3)]
    line = pick(total, 1, y, 0).astype(F32) + sum(g.astype(F32) for g in got)
    got = [fetch(pick(line, 0, x, k).astype(BF16), "x", SIDE, -k) for k in (1, 2, 3)]
    return pick(line, 0, x, 0) + sum(g.astype(F32) for g in got)


def scatter_cols(part):
    me = lax.axis_index("col")
    rows = part.shape[1] // RING

    def block(offset):
        start = lax.rem(me + offset + RING, RING) * rows
        return lax.dynamic_slice_in_dim(part, start, rows, 1)

    def halves(value):
        if value.shape[0] == 2:
            return value[:1], value[1:], 0
        return value[:, : rows // 2], value[:, rows // 2 :], 1

    low, high, axis = halves(block(4))
    low, high = fetch(low, "col", RING, -2), fetch(high, "col", RING, 2)
    up, down = fetch(block(3), "col", RING, -1), fetch(block(-3), "col", RING, 1)
    near_up, near_down = fetch(block(1), "col", RING, -1), fetch(block(-1), "col", RING, 1)
    up = block(2).astype(F32) + up.astype(F32)
    down = block(-2).astype(F32) + down.astype(F32)
    a, b, _ = halves(up)
    up = jnp.concatenate([a + low.astype(F32), b], axis)
    a, b, _ = halves(down)
    down = jnp.concatenate([a, b + high.astype(F32)], axis)
    up, down = fetch(up.astype(BF16), "col", RING, -2), fetch(down.astype(BF16), "col", RING, 2)
    near = block(0).astype(F32) + near_up.astype(F32) + near_down.astype(F32)
    return near + up.astype(F32) + down.astype(F32)


def gather_cols(value):
    me = lax.axis_index("col")
    rows = value.shape[0]
    half = rows // 2
    up2, down2 = fetch(value, "col", RING, 2), fetch(value, "col", RING, -2)
    up1, down1 = fetch(value, "col", RING, 1), fetch(value, "col", RING, -1)
    low, high = fetch(up2[:half], "col", RING, 2), fetch(down2[half:], "col", RING, -2)
    up3, down3 = fetch(up2, "col", RING, 1), fetch(down2, "col", RING, -1)
    out = jnp.zeros((RING * rows,) + value.shape[1:], value.dtype)
    pieces = [(value, 0, 0), (up1, 1, 0), (down1, -1, 0), (up2, 2, 0), (down2, -2, 0)]
    pieces += [(up3, 3, 0), (down3, -3, 0), (low, 4, 0), (high, 4, half)]
    for piece, offset, start in pieces:
        at = lax.rem(me + offset + RING, RING) * rows + start
        out = lax.dynamic_update_slice_in_dim(out, piece, at, 0)
    return out


def per_device(tokens, gate_up, down, target):
    all_tokens = gather_rows(tokens)
    half = all_tokens.shape[0] // 2
    partial_value = jnp.einsum("td,dgf->gtf", all_tokens, gate_up, preferred_element_type=F32).astype(BF16)
    projected = scatter_cols(partial_value)
    gate, up = projected[0], projected[1]
    hidden = (gate * jax.nn.sigmoid(gate) * up).astype(BF16)
    all_hidden = gather_cols(hidden)
    all_hidden, projected = lax.optimization_barrier((all_hidden, projected.astype(BF16)))
    all_projected = lax.all_gather(projected, "col", axis=1, tiled=True)
    other = jnp.dot(all_hidden[half:], down, preferred_element_type=F32).astype(BF16)
    own = jnp.dot(all_hidden[:half], down, preferred_element_type=F32)
    mixed = scatter_rows(own, other)
    output = (tokens.astype(F32) + mixed).astype(BF16)
    delta = (output.astype(F32) - target.astype(F32)).astype(BF16)
    all_delta = gather_rows(delta)
    hidden_part = jnp.einsum("td,fd->tf", all_delta, down, preferred_element_type=F32).astype(BF16)
    grad_hidden = scatter_cols(hidden_part[None])[0]
    grad_down = jnp.einsum("tf,td->fd", all_hidden, all_delta, preferred_element_type=F32).astype(BF16)
    grad_hidden = grad_hidden.astype(BF16)
    grad_hidden, all_projected, grad_down = lax.optimization_barrier((grad_hidden, all_projected, grad_down))
    all_grad_hidden = gather_cols(grad_hidden).astype(F32)
    all_gate, all_up = all_projected[0].astype(F32), all_projected[1].astype(F32)
    sigma = jax.nn.sigmoid(all_gate)
    grad_gate = all_grad_hidden * all_up * sigma * (1.0 + all_gate * (1.0 - sigma))
    grad_up = all_grad_hidden * all_gate * sigma
    all_grad = jnp.stack([grad_gate, grad_up], 0).astype(BF16)

    inner = jnp.einsum("gtf,dgf->td", all_grad, gate_up, preferred_element_type=F32).astype(BF16)
    grad_inner = scatter_rows_in_steps(inner[:half].astype(F32), inner[half:])
    grad_gate_up = jnp.einsum("td,gtf->dgf", all_tokens, all_grad, preferred_element_type=F32).astype(BF16)
    grad_tokens = (delta.astype(F32) + grad_inner).astype(BF16)
    return (output, grad_tokens, grad_gate_up, grad_down)


def solution(mesh):
    chips = Mesh(mesh.devices.reshape(SIDE, SIDE, 2, RING), ROW + ("col",))
    in_specs = (P(ROW, "col"), P("col", None, ROW), P(ROW, "col"), P(ROW, "col"))
    out_specs = (P(ROW, "col"), P(ROW, "col"), P("col", None, ROW), P(ROW, "col"))
    return jax.shard_map(
        per_device, mesh=chips, in_specs=in_specs, out_specs=out_specs, check_vma=False
    )
```

```python
import jax
import jax.numpy as jnp
from jax import lax
from jax.sharding import Mesh
from jax.sharding import PartitionSpec as P

BF16 = jnp.bfloat16
F32 = jnp.float32
ROW = ("x", "y", "core")
PLANE = ("x", "y")
SIDE = 4
RING = 8


def fetch(value, axis, size, offset):
    return lax.ppermute(value, axis, [((i + offset) % size, i) for i in range(size)])


def swap_core(value):
    return lax.ppermute(value, "core", [(0, 1), (1, 0)])


def gather(value, axes, size):
    copies = jnp.broadcast_to(value[None], (size,) + value.shape).reshape((-1,) + value.shape[1:])
    return lax.all_to_all(copies, axes, 0, 0, tiled=True)


def gather_rows(value):
    own = gather(value, PLANE, SIDE * SIDE)
    return own, swap_core(own)


def scatter_rows(own, other):
    got = swap_core(other.astype(BF16))
    own, got = lax.optimization_barrier((own, got))
    total = (own + got.astype(F32)).astype(BF16)
    got = lax.all_to_all(total, PLANE, 0, 0, tiled=True)
    return jnp.sum(got.reshape((SIDE * SIDE, -1) + got.shape[1:]).astype(F32), 0)


def scatter_cols(part):
    me = lax.axis_index("col")
    rows = part.shape[1] // RING

    def block(offset):
        start = lax.rem(me + offset + RING, RING) * rows
        return lax.dynamic_slice_in_dim(part, start, rows, 1)

    def halves(value):
        if value.shape[0] == 2:
            return value[:1], value[1:], 0
        return value[:, : rows // 2], value[:, rows // 2 :], 1

    low, high, axis = halves(block(4))
    low, high = fetch(low, "col", RING, -2), fetch(high, "col", RING, 2)
    up, down = fetch(block(3), "col", RING, -1), fetch(block(-3), "col", RING, 1)
    near_up, near_down = fetch(block(1), "col", RING, -1), fetch(block(-1), "col", RING, 1)
    up = block(2).astype(F32) + up.astype(F32)
    down = block(-2).astype(F32) + down.astype(F32)
    a, b, _ = halves(up)
    up = jnp.concatenate([a + low.astype(F32), b], axis)
    a, b, _ = halves(down)
    down = jnp.concatenate([a, b + high.astype(F32)], axis)
    up, down = fetch(up.astype(BF16), "col", RING, -2), fetch(down.astype(BF16), "col", RING, 2)
    near = block(0).astype(F32) + near_up.astype(F32) + near_down.astype(F32)
    return near + up.astype(F32) + down.astype(F32)


def gather_cols(value):
    me = lax.axis_index("col")
    rows = value.shape[0]
    half = rows // 2
    up2, down2 = fetch(value, "col", RING, 2), fetch(value, "col", RING, -2)
    up1, down1 = fetch(value, "col", RING, 1), fetch(value, "col", RING, -1)
    low, high = fetch(up2[:half], "col", RING, 2), fetch(down2[half:], "col", RING, -2)
    up3, down3 = fetch(up2, "col", RING, 1), fetch(down2, "col", RING, -1)
    out = jnp.zeros((RING * rows,) + value.shape[1:], value.dtype)
    pieces = [(value, 0, 0), (up1, 1, 0), (down1, -1, 0), (up2, 2, 0), (down2, -2, 0)]
    pieces += [(up3, 3, 0), (down3, -3, 0), (low, 4, 0), (high, 4, half)]
    for piece, offset, start in pieces:
        at = lax.rem(me + offset + RING, RING) * rows + start
        out = lax.dynamic_update_slice_in_dim(out, piece, at, 0)
    return out


def per_device(tokens, gate_up, down, target):
    own_tokens, other_tokens = gather_rows(tokens)
    half = own_tokens.shape[0]
    all_tokens = jnp.concatenate([own_tokens, other_tokens], 0)
    partial_value = jnp.einsum("td,dgf->gtf", all_tokens, gate_up, preferred_element_type=F32).astype(BF16)
    projected = scatter_cols(partial_value)
    gate, up = projected[0], projected[1]
    hidden = (gate * jax.nn.sigmoid(gate) * up).astype(BF16)
    all_hidden = gather_cols(hidden)
    all_hidden, projected = lax.optimization_barrier((all_hidden, projected.astype(BF16)))
    all_projected = lax.all_gather(projected, "col", axis=1, tiled=True)
    other = jnp.dot(all_hidden[half:], down, preferred_element_type=F32)
    own = jnp.dot(all_hidden[:half], down, preferred_element_type=F32)
    mixed = scatter_rows(own, other)
    output = (tokens.astype(F32) + mixed).astype(BF16)
    delta = (output.astype(F32) - target.astype(F32)).astype(BF16)
    all_delta = jnp.concatenate(gather_rows(delta), 0)
    hidden_part = jnp.einsum("td,fd->tf", all_delta, down, preferred_element_type=F32).astype(BF16)
    grad_hidden = scatter_cols(hidden_part[None])[0]
    grad_down = jnp.einsum("tf,td->fd", all_hidden, all_delta, preferred_element_type=F32).astype(BF16)
    grad_hidden = grad_hidden.astype(BF16)
    grad_hidden, all_projected, grad_down, own_tokens, other_tokens = lax.optimization_barrier(
        (grad_hidden, all_projected, grad_down, own_tokens, other_tokens)
    )
    all_grad_hidden = gather_cols(grad_hidden).astype(F32)
    all_gate, all_up = all_projected[0].astype(F32), all_projected[1].astype(F32)
    sigma = jax.nn.sigmoid(all_gate)
    grad_gate = all_grad_hidden * all_up * sigma * (1.0 + all_gate * (1.0 - sigma))
    grad_up = all_grad_hidden * all_gate * sigma
    all_grad = jnp.stack([grad_gate, grad_up], 0).astype(BF16)

    def inner(grad):
        return jnp.einsum("gtf,dgf->td", grad, gate_up, preferred_element_type=F32)

    other, own = inner(all_grad[:, half:]), inner(all_grad[:, :half])
    grad_inner = scatter_rows(own, other)
    all_tokens = jnp.concatenate([own_tokens, other_tokens], 0)
    grad_gate_up = jnp.einsum("td,gtf->dgf", all_tokens, all_grad, preferred_element_type=F32).astype(BF16)
    grad_tokens = (delta.astype(F32) + grad_inner).astype(BF16)
    return (output, grad_tokens, grad_gate_up, grad_down)


def solution(mesh):
    chips = Mesh(mesh.devices.reshape(SIDE, SIDE, 2, RING), ROW + ("col",))
    in_specs = (P(ROW, "col"), P("col", None, ROW), P(ROW, "col"), P(ROW, "col"))
    out_specs = (P(ROW, "col"), P(ROW, "col"), P("col", None, ROW), P(ROW, "col"))
    return jax.shard_map(
        per_device, mesh=chips, in_specs=in_specs, out_specs=out_specs, check_vma=False
    )
```

```python
import jax
import jax.numpy as jnp
from jax import lax
from jax.sharding import Mesh
from jax.sharding import PartitionSpec as P

BF16 = jnp.bfloat16
F32 = jnp.float32
ROW = ("x", "y", "core")
PLANE = ("x", "y")
SIDE = 4
RING = 8


def fetch(value, axis, size, offset):
    return lax.ppermute(value, axis, [((i + offset) % size, i) for i in range(size)])


def swap_core(value):
    return lax.ppermute(value, "core", [(0, 1), (1, 0)])


def gather(value, axes, size):
    copies = jnp.broadcast_to(value[None], (size,) + value.shape).reshape((-1,) + value.shape[1:])
    return lax.all_to_all(copies, axes, 0, 0, tiled=True)


def gather_rows(value):
    own = gather(value, PLANE, SIDE * SIDE)
    return own, swap_core(own)


def scatter_rows(own, other):
    got = swap_core(other.astype(BF16))
    own, got = lax.optimization_barrier((own, got))
    total = (own + got.astype(F32)).astype(BF16)
    got = lax.all_to_all(total, PLANE, 0, 0, tiled=True)
    return jnp.sum(got.reshape((SIDE * SIDE, -1) + got.shape[1:]).astype(F32), 0)


def places(rows):
    me = lax.axis_index("col")
    ahead = [lax.rem(me + offset, RING) for offset in range(RING)]
    twice = [2 * place for place in ahead]
    return [place * rows for place in ahead], twice + [twice[RING // 2] + 1]


def scatter_cols(part, starts):
    rows = part.shape[1] // RING

    def block(offset):
        return lax.dynamic_slice_in_dim(part, starts[offset % RING], rows, 1, allow_negative_indices=False)

    def halves(value):
        if value.shape[0] == 2:
            return value[:1], value[1:], 0
        return value[:, : rows // 2], value[:, rows // 2 :], 1

    low, high, axis = halves(block(4))
    low, high = fetch(low, "col", RING, -2), fetch(high, "col", RING, 2)
    up, down = fetch(block(3), "col", RING, -1), fetch(block(-3), "col", RING, 1)
    near_up, near_down = fetch(block(1), "col", RING, -1), fetch(block(-1), "col", RING, 1)
    up = block(2).astype(F32) + up.astype(F32)
    down = block(-2).astype(F32) + down.astype(F32)
    a, b, _ = halves(up)
    up = jnp.concatenate([a + low.astype(F32), b], axis)
    a, b, _ = halves(down)
    down = jnp.concatenate([a, b + high.astype(F32)], axis)
    up, down = fetch(up.astype(BF16), "col", RING, -2), fetch(down.astype(BF16), "col", RING, 2)
    near = block(0).astype(F32) + near_up.astype(F32) + near_down.astype(F32)
    return near + up.astype(F32) + down.astype(F32)


def gather_cols(value, twice):
    rows = value.shape[0]
    half = rows // 2
    up2, down2 = fetch(value, "col", RING, 2), fetch(value, "col", RING, -2)
    up1, down1 = fetch(value, "col", RING, 1), fetch(value, "col", RING, -1)
    low, high = fetch(up2[:half], "col", RING, 2), fetch(down2[half:], "col", RING, -2)
    up3, down3 = fetch(up2, "col", RING, 1), fetch(down2, "col", RING, -1)
    out = jnp.zeros((2 * RING, half) + value.shape[1:], value.dtype)
    pieces = [(value, 0), (up1, 1), (down1, 7), (up2, 2), (down2, 6), (up3, 3), (down3, 5), (low, 4), (high, RING)]
    for piece, at in pieces:
        piece = piece.reshape((-1,) + out.shape[1:])
        out = lax.dynamic_update_slice_in_dim(out, piece, twice[at], 0, allow_negative_indices=False)
    return out.reshape((RING * rows,) + value.shape[1:])


def per_device(tokens, gate_up, down, target):
    rows = tokens.shape[0] * 2 * SIDE * SIDE // RING
    tokens, (starts, twice) = lax.optimization_barrier((tokens, places(rows)))
    own_tokens, other_tokens = gather_rows(tokens)
    half = own_tokens.shape[0]
    all_tokens = jnp.concatenate([own_tokens, other_tokens], 0)
    partial_value = jnp.einsum("td,dgf->gtf", all_tokens, gate_up, preferred_element_type=F32).astype(BF16)
    projected = scatter_cols(partial_value, starts)
    gate, up = projected[0], projected[1]
    hidden = (gate * jax.nn.sigmoid(gate) * up).astype(BF16)
    all_hidden = gather_cols(hidden, twice)
    all_hidden, projected = lax.optimization_barrier((all_hidden, projected.astype(BF16)))
    all_projected = lax.all_gather(projected, "col", axis=1, tiled=True)
    other = jnp.dot(all_hidden[half:], down, preferred_element_type=F32)
    own = jnp.dot(all_hidden[:half], down, preferred_element_type=F32)
    mixed = scatter_rows(own, other)
    output = (tokens.astype(F32) + mixed).astype(BF16)
    delta = (output.astype(F32) - target.astype(F32)).astype(BF16)
    all_delta = jnp.concatenate(gather_rows(delta), 0)
    hidden_part = jnp.einsum("td,fd->tf", all_delta, down, preferred_element_type=F32).astype(BF16)
    grad_hidden = scatter_cols(hidden_part[None], starts)[0]
    grad_down = jnp.einsum("tf,td->fd", all_hidden, all_delta, preferred_element_type=F32).astype(BF16)
    grad_hidden = grad_hidden.astype(BF16)
    grad_hidden, all_projected, grad_down, own_tokens, other_tokens = lax.optimization_barrier(
        (grad_hidden, all_projected, grad_down, own_tokens, other_tokens)
    )
    all_grad_hidden = gather_cols(grad_hidden, twice).astype(F32)
    all_gate, all_up = all_projected[0].astype(F32), all_projected[1].astype(F32)
    sigma = jax.nn.sigmoid(all_gate)
    grad_gate = all_grad_hidden * all_up * sigma * (1.0 + all_gate * (1.0 - sigma))
    grad_up = all_grad_hidden * all_gate * sigma
    all_grad = jnp.stack([grad_gate, grad_up], 0).astype(BF16)

    def inner(grad):
        return jnp.einsum("gtf,dgf->td", grad, gate_up, preferred_element_type=F32)

    other, own = inner(all_grad[:, half:]), inner(all_grad[:, :half])
    grad_inner = scatter_rows(own, other)
    all_tokens = jnp.concatenate([own_tokens, other_tokens], 0)
    grad_gate_up = jnp.einsum("td,gtf->dgf", all_tokens, all_grad, preferred_element_type=F32).astype(BF16)
    grad_tokens = (delta.astype(F32) + grad_inner).astype(BF16)
    return (output, grad_tokens, grad_gate_up, grad_down)


def solution(mesh):
    chips = Mesh(mesh.devices.reshape(SIDE, SIDE, 2, RING), ROW + ("col",))
    in_specs = (P(ROW, "col"), P("col", None, ROW), P(ROW, "col"), P(ROW, "col"))
    out_specs = (P(ROW, "col"), P(ROW, "col"), P("col", None, ROW), P(ROW, "col"))
    return jax.shard_map(
        per_device, mesh=chips, in_specs=in_specs, out_specs=out_specs, check_vma=False
    )
```

```python
import jax
import jax.numpy as jnp
from jax import lax
from jax.experimental import pallas as pl
from jax.experimental.pallas import tpu as pltpu
from jax.sharding import Mesh
from jax.sharding import PartitionSpec as P

BF16 = jnp.bfloat16
F32 = jnp.float32
ROW = ("x", "y", "core")
PLANE = ("x", "y")
SIDE = 4
RING = 8


def hand_on(source, target):
    del source, target


def in_vmem(value):
    return pl.pallas_call(
        hand_on,
        out_shape=jax.ShapeDtypeStruct(value.shape, value.dtype),
        in_specs=[pl.BlockSpec(memory_space=pltpu.VMEM)],
        out_specs=pl.BlockSpec(memory_space=pltpu.VMEM),
        input_output_aliases={0: 0},
        compiler_params=pltpu.CompilerParams(vmem_limit_bytes=2**20),
    )(value)


def fetch(value, axis, size, offset):
    return lax.ppermute(value, axis, [((i + offset) % size, i) for i in range(size)])


def swap_core(value):
    return lax.ppermute(value, "core", [(0, 1), (1, 0)])


def gather(value, axes, size):
    copies = jnp.broadcast_to(value[None], (size,) + value.shape).reshape((-1,) + value.shape[1:])
    return lax.all_to_all(copies, axes, 0, 0, tiled=True)


def gather_rows(value):
    own = gather(value, PLANE, SIDE * SIDE)
    return own, swap_core(own)


def scatter_rows(own, other):
    got = swap_core(other.astype(BF16))
    own, got = lax.optimization_barrier((own, got))
    total = (own + got.astype(F32)).astype(BF16)
    got = lax.all_to_all(total, PLANE, 0, 0, tiled=True)
    return jnp.sum(got.reshape((SIDE * SIDE, -1) + got.shape[1:]).astype(F32), 0)


def places(rows):
    me = lax.axis_index("col")
    ahead = [lax.rem(me + offset, RING) for offset in range(RING)]
    twice = [2 * place for place in ahead]
    return [place * rows for place in ahead], twice + [twice[RING // 2] + 1]


def scatter_cols(part, starts):
    rows = part.shape[1] // RING

    def block(offset):
        return lax.dynamic_slice_in_dim(part, starts[offset % RING], rows, 1, allow_negative_indices=False)

    def halves(value):
        if value.shape[0] == 2:
            return value[:1], value[1:], 0
        return value[:, : rows // 2], value[:, rows // 2 :], 1

    low, high, axis = halves(block(4))
    low, high = fetch(low, "col", RING, -2), fetch(high, "col", RING, 2)
    up, down = fetch(block(3), "col", RING, -1), fetch(block(-3), "col", RING, 1)
    near_up, near_down = fetch(block(1), "col", RING, -1), fetch(block(-1), "col", RING, 1)
    up = block(2).astype(F32) + up.astype(F32)
    down = block(-2).astype(F32) + down.astype(F32)
    a, b, _ = halves(up)
    up = jnp.concatenate([a + low.astype(F32), b], axis)
    a, b, _ = halves(down)
    down = jnp.concatenate([a, b + high.astype(F32)], axis)
    up, down = fetch(up.astype(BF16), "col", RING, -2), fetch(down.astype(BF16), "col", RING, 2)
    near = block(0).astype(F32) + near_up.astype(F32) + near_down.astype(F32)
    return near + up.astype(F32) + down.astype(F32)


def gather_cols(value, twice):
    rows = value.shape[0]
    half = rows // 2
    up2, down2 = fetch(value, "col", RING, 2), fetch(value, "col", RING, -2)
    up1, down1 = fetch(value, "col", RING, 1), fetch(value, "col", RING, -1)
    low, high = fetch(up2[:half], "col", RING, 2), fetch(down2[half:], "col", RING, -2)
    up3, down3 = fetch(up2, "col", RING, 1), fetch(down2, "col", RING, -1)
    out = jnp.zeros((2 * RING, half) + value.shape[1:], value.dtype)
    pieces = [(value, 0), (up2, 2), (down2, 6), (up1, 1), (down1, 7), (low, 4), (high, RING), (up3, 3), (down3, 5)]
    for piece, at in pieces:
        piece = piece.reshape((-1,) + out.shape[1:])
        out = lax.dynamic_update_slice_in_dim(out, piece, twice[at], 0, allow_negative_indices=False)
    return out.reshape((RING * rows,) + value.shape[1:])


def per_device(tokens, gate_up, down, target):
    rows = tokens.shape[0] * 2 * SIDE * SIDE // RING
    tokens, (starts, twice) = lax.optimization_barrier((tokens, places(rows)))
    own_tokens, other_tokens = gather_rows(tokens)
    half = own_tokens.shape[0]
    all_tokens = jnp.concatenate([own_tokens, other_tokens], 0)
    partial_value = jnp.einsum("td,dgf->gtf", all_tokens, in_vmem(gate_up), preferred_element_type=F32).astype(BF16)
    projected = scatter_cols(partial_value, starts)
    gate, up = projected[0], projected[1]
    hidden = (gate * jax.nn.sigmoid(gate) * up).astype(BF16)
    all_hidden = gather_cols(hidden, twice)
    all_hidden, projected = lax.optimization_barrier((all_hidden, projected.astype(BF16)))
    all_projected = lax.all_gather(projected, "col", axis=1, tiled=True)
    other = jnp.dot(all_hidden[half:], down, preferred_element_type=F32)
    own = jnp.dot(all_hidden[:half], down, preferred_element_type=F32)
    mixed = scatter_rows(own, other)
    output = (tokens.astype(F32) + mixed).astype(BF16)
    delta = (output.astype(F32) - target.astype(F32)).astype(BF16)
    all_delta = jnp.concatenate(gather_rows(delta), 0)
    hidden_part = jnp.einsum("td,fd->tf", all_delta, down, preferred_element_type=F32).astype(BF16)
    grad_hidden = scatter_cols(hidden_part[None], starts)[0]
    grad_down = jnp.einsum("tf,td->fd", all_hidden, all_delta, preferred_element_type=F32).astype(BF16)
    grad_hidden = grad_hidden.astype(BF16)
    grad_hidden, all_projected, grad_down, own_tokens, other_tokens = lax.optimization_barrier(
        (grad_hidden, all_projected, grad_down, own_tokens, other_tokens)
    )
    all_grad_hidden = gather_cols(grad_hidden, twice).astype(F32)
    all_gate, all_up = all_projected[0].astype(F32), all_projected[1].astype(F32)
    sigma = jax.nn.sigmoid(all_gate)
    grad_gate = all_grad_hidden * all_up * sigma * (1.0 + all_gate * (1.0 - sigma))
    grad_up = all_grad_hidden * all_gate * sigma
    all_grad = jnp.stack([grad_gate, grad_up], 0).astype(BF16)

    def inner(grad):
        return jnp.einsum("gtf,dgf->td", grad, gate_up, preferred_element_type=F32)

    other, own = inner(all_grad[:, half:]), inner(all_grad[:, :half])
    grad_inner = scatter_rows(own, other)
    all_tokens = jnp.concatenate([own_tokens, other_tokens], 0)
    grad_gate_up = jnp.einsum("td,gtf->dgf", all_tokens, all_grad, preferred_element_type=F32).astype(BF16)
    grad_tokens = (delta.astype(F32) + grad_inner).astype(BF16)
    return (output, grad_tokens, grad_gate_up, grad_down)


def solution(mesh):
    chips = Mesh(mesh.devices.reshape(SIDE, SIDE, 2, RING), ROW + ("col",))
    in_specs = (P(ROW, "col"), P("col", None, ROW), P(ROW, "col"), P(ROW, "col"))
    out_specs = (P(ROW, "col"), P(ROW, "col"), P("col", None, ROW), P(ROW, "col"))
    return jax.shard_map(
        per_device, mesh=chips, in_specs=in_specs, out_specs=out_specs, check_vma=False
    )
```

```python
import jax
import jax.numpy as jnp
from jax import lax
from jax.experimental import pallas as pl
from jax.experimental.pallas import tpu as pltpu
from jax.sharding import Mesh
from jax.sharding import PartitionSpec as P

BF16 = jnp.bfloat16
F32 = jnp.float32
ROW = ("x", "y", "core")
PLANE = ("x", "y")
SIDE = 4
RING = 8


def hand_on(source, target):
    del source, target


def in_vmem(value):
    return pl.pallas_call(
        hand_on,
        out_shape=jax.ShapeDtypeStruct(value.shape, value.dtype),
        in_specs=[pl.BlockSpec(memory_space=pltpu.VMEM)],
        out_specs=pl.BlockSpec(memory_space=pltpu.VMEM),
        input_output_aliases={0: 0},
        compiler_params=pltpu.CompilerParams(vmem_limit_bytes=2**20),
    )(value)


def fetch(value, axis, size, offset):
    return lax.ppermute(value, axis, [((i + offset) % size, i) for i in range(size)])


def swap_core(value):
    return lax.ppermute(value, "core", [(0, 1), (1, 0)])


def gather(value, axes, size):
    copies = jnp.broadcast_to(value[None], (size,) + value.shape).reshape((-1,) + value.shape[1:])
    return lax.all_to_all(copies, axes, 0, 0, tiled=True)


def gather_rows(value):
    own = gather(value, PLANE, SIDE * SIDE)
    return own, swap_core(own)


def scatter_rows(own, other):
    got = swap_core(other.astype(BF16))
    own, got = lax.optimization_barrier((own, got))
    total = (own + got.astype(F32)).astype(BF16)
    got = lax.all_to_all(total, PLANE, 0, 0, tiled=True)
    return jnp.sum(got.reshape((SIDE * SIDE, -1) + got.shape[1:]).astype(F32), 0)


def places(rows):
    me = lax.axis_index("col")
    ahead = [lax.rem(me + offset, RING) for offset in range(RING)]
    twice = [2 * place for place in ahead]
    return [place * rows for place in ahead], twice + [twice[RING // 2] + 1]


def scatter_cols(part, starts):
    rows = part.shape[1] // RING

    def block(offset):
        return lax.dynamic_slice_in_dim(part, starts[offset % RING], rows, 1, allow_negative_indices=False)

    def halves(value):
        if value.shape[0] == 2:
            return value[:1], value[1:], 0
        return value[:, : rows // 2], value[:, rows // 2 :], 1

    low, high, axis = halves(block(4))
    low, high = fetch(low, "col", RING, -2), fetch(high, "col", RING, 2)
    up, down = fetch(block(3), "col", RING, -1), fetch(block(-3), "col", RING, 1)
    near_up, near_down = fetch(block(1), "col", RING, -1), fetch(block(-1), "col", RING, 1)
    up = block(2).astype(F32) + up.astype(F32)
    down = block(-2).astype(F32) + down.astype(F32)
    a, b, _ = halves(up)
    up = jnp.concatenate([a + low.astype(F32), b], axis)
    a, b, _ = halves(down)
    down = jnp.concatenate([a, b + high.astype(F32)], axis)
    up, down = fetch(up.astype(BF16), "col", RING, -2), fetch(down.astype(BF16), "col", RING, 2)
    near = block(0).astype(F32) + near_up.astype(F32) + near_down.astype(F32)
    return near + up.astype(F32) + down.astype(F32)


def gather_cols(value, twice):
    rows = value.shape[0]
    half = rows // 2
    up2, down2 = fetch(value, "col", RING, 2), fetch(value, "col", RING, -2)
    up1, down1 = fetch(value, "col", RING, 1), fetch(value, "col", RING, -1)
    low, high = fetch(up2[:half], "col", RING, 2), fetch(down2[half:], "col", RING, -2)
    up3, down3 = fetch(up2, "col", RING, 1), fetch(down2, "col", RING, -1)
    out = jnp.zeros((2 * RING, half) + value.shape[1:], value.dtype)
    pieces = [(value, 0), (low, 4), (high, RING), (up3, 3), (down3, 5), (up2, 2), (down2, 6), (up1, 1), (down1, 7)]
    for piece, at in pieces:
        piece = piece.reshape((-1,) + out.shape[1:])
        out = lax.dynamic_update_slice_in_dim(out, piece, twice[at], 0, allow_negative_indices=False)
    return out.reshape((RING * rows,) + value.shape[1:])


def per_device(tokens, gate_up, down, target):
    rows = tokens.shape[0] * 2 * SIDE * SIDE // RING
    tokens, (starts, twice) = lax.optimization_barrier((tokens, places(rows)))
    own_tokens, other_tokens = gather_rows(tokens)
    half = own_tokens.shape[0]
    all_tokens = jnp.concatenate([own_tokens, other_tokens], 0)
    partial_value = jnp.einsum("td,dgf->gtf", all_tokens, in_vmem(gate_up), preferred_element_type=F32).astype(BF16)
    projected = scatter_cols(partial_value, starts)
    gate, up = projected[0], projected[1]
    hidden = (gate * jax.nn.sigmoid(gate) * up).astype(BF16)
    all_hidden = gather_cols(hidden, twice)
    all_hidden, projected = lax.optimization_barrier((all_hidden, projected.astype(BF16)))
    all_projected = lax.all_gather(projected, "col", axis=1, tiled=True)
    other = jnp.dot(all_hidden[half:], down, preferred_element_type=F32)
    own = jnp.dot(all_hidden[:half], down, preferred_element_type=F32)
    mixed = scatter_rows(own, other)
    output = (tokens.astype(F32) + mixed).astype(BF16)
    delta = (output.astype(F32) - target.astype(F32)).astype(BF16)
    all_delta = jnp.concatenate(gather_rows(delta), 0)
    hidden_part = jnp.einsum("td,fd->tf", all_delta, down, preferred_element_type=F32).astype(BF16)
    grad_hidden = scatter_cols(hidden_part[None], starts)[0]
    grad_down = jnp.einsum("tf,td->fd", all_hidden, all_delta, preferred_element_type=F32).astype(BF16)
    grad_hidden = grad_hidden.astype(BF16)
    grad_hidden, all_projected, grad_down, own_tokens, other_tokens = lax.optimization_barrier(
        (grad_hidden, all_projected, grad_down, own_tokens, other_tokens)
    )
    all_grad_hidden = gather_cols(grad_hidden, twice).astype(F32)
    all_gate, all_up = all_projected[0].astype(F32), all_projected[1].astype(F32)
    sigma = jax.nn.sigmoid(all_gate)
    grad_gate = all_grad_hidden * all_up * sigma * (1.0 + all_gate * (1.0 - sigma))
    grad_up = all_grad_hidden * all_gate * sigma
    all_grad = jnp.stack([grad_gate, grad_up], 0).astype(BF16)

    def inner(grad):
        return jnp.einsum("gtf,dgf->td", grad, gate_up, preferred_element_type=F32)

    other, own = inner(all_grad[:, half:]), inner(all_grad[:, :half])
    grad_inner = scatter_rows(own, other)
    all_tokens = jnp.concatenate([own_tokens, other_tokens], 0)
    grad_gate_up = jnp.einsum("td,gtf->dgf", all_tokens, all_grad, preferred_element_type=F32).astype(BF16)
    grad_tokens = (delta.astype(F32) + grad_inner).astype(BF16)
    return (output, grad_tokens, grad_gate_up, grad_down)


def solution(mesh):
    chips = Mesh(mesh.devices.reshape(SIDE, SIDE, 2, RING), ROW + ("col",))
    in_specs = (P(ROW, "col"), P("col", None, ROW), P(ROW, "col"), P(ROW, "col"))
    out_specs = (P(ROW, "col"), P(ROW, "col"), P("col", None, ROW), P(ROW, "col"))
    return jax.shard_map(
        per_device, mesh=chips, in_specs=in_specs, out_specs=out_specs, check_vma=False
    )
```
